32 devices in a mesh: groups: 2 (over y), blk: 4 (over z), layer: 2 (over x), rep: 2 (over core).
Axes of the slice: x: 2, y: 2, z: 4, core: 2. Of those that a mesh axis runs over, the one named last changes fastest.
Arguments:
- train_grads: bfloat16 [2, 8192, 4096], P('layer', ('groups', 'blk')), parts along dimension 1, may hold values from -0.29882812 to 0.29882812
- queries: bfloat16 [2, 2, 512, 4096], P('layer', 'rep', ('groups', 'blk')), parts along dimension 2, may hold values from -0.59765625 to 0.59765625
- bases: bfloat16 [2, 64, 128], P('layer', ('blk', 'rep')), may hold values from -0.75 to 0.75
- eigenvalues: float32 [2, 4096], P('layer', ('blk', 'rep')), may hold values from 0.01 to 10
Outputs:
- scores: float32 [2, 256, 8192], P('rep', 'layer', ('groups', 'blk')), parts along dimension 2
The draws below stay inside these ranges and needn't reach their ends.
There are 2 independent parts, one for each index of `groups`. The reference program is written for one: setup_inputs(seed, part) draws one part's arguments, and reference() takes and returns one part's arrays. A program takes and returns all parts, laid end to end along the dimension named above; an argument that names none is the same for every part. Nothing has to cross between parts.
All inputs are finite; a program needn't handle non-finite values.
Results may differ from the reference program's by a relative error of at most 0.0042.
Values may be sent and summed in bfloat16 or wider, within the bound.
A program may use at most 128 MiB of HBM per device.

```python
import math
import jax
import jax.numpy as jnp
from jax import lax

K = 64
P_SIZE = 4096
L = 2
QH = 256
NT = 4096
N_REP = 2


def block_scale(key, extent, split, low, top_value):
    def one(axis_at, blocks):
        draws = jax.random.uniform(jax.random.fold_in(jax.random.fold_in(key, 6), axis_at), (blocks,), jnp.float32, low / len(split), top_value / len(split))
        return jnp.repeat(jnp.exp(draws), extent[axis_at] // blocks).reshape((-1,) + (1,) * (len(extent) - axis_at - 1))

    loudness = one(*split[0])
    for cut in split[1:]:
        loudness = loudness * one(*cut)
    return loudness


def scatter_about(stream_key, extent, width, limit, split=(), held_as=jnp.bfloat16):
    values = width * jax.random.normal(stream_key, extent, jnp.float32)
    if split:
        values = values * block_scale(stream_key, extent, split, -0.22, 0.18)
    return jnp.clip(values, -limit, limit).astype(held_as)


def setup_inputs(seed: int = 0, part: int = 0) -> dict:
    keys = jax.random.split(jax.random.key(seed), 5)
    part_splits = jax.random.split(jax.random.fold_in(keys[4], part), 5)
    train_grads = scatter_about(part_splits[0], (L, NT, P_SIZE), 0.05, 0.29882812, ((0, 2), (1, 4)))
    queries = scatter_about(part_splits[1], (L, N_REP, QH, P_SIZE), 0.1, 0.59765625, ((0, 2), (1, 2), (2, 4)))
    bases = scatter_about(keys[2], (L, K, 2 * K), K ** -0.5, 0.75, ((0, 2), (1, 8)))
    eigenvalues = jnp.clip(jnp.exp(math.log(10.0) - 6.9077553 * jax.random.uniform(keys[3], (L, P_SIZE), jnp.float32) ** block_scale(keys[3], (L, P_SIZE), ((0, 2), (1, 8)), -0.2, 0.2)), 0.01, 10.0)
    return {"train_grads": train_grads, "queries": queries, "bases": bases, "eigenvalues": eigenvalues}


def rotate_rows(grads, basis):
    factor_size = basis.shape[0]
    row_count = grads.shape[0]
    grad_square = grads.astype(jnp.float32).reshape(row_count, factor_size, factor_size)
    right_basis = basis[:, factor_size:].astype(jnp.float32)
    left_basis = basis[:, :factor_size].astype(jnp.float32)
    half_turn = jnp.einsum('rab,bc->rac', grad_square, right_basis).astype(jnp.bfloat16)
    half_turn = lax.optimization_barrier(half_turn)
    full_turn = jnp.einsum('ca,rcb->rab', left_basis, half_turn.astype(jnp.float32))
    return full_turn.reshape(row_count, factor_size * factor_size)


def reference(train_grads, queries, bases, eigenvalues):
    layer_count = train_grads.shape[0]
    query_rows = queries.reshape(layer_count, queries.shape[1] * queries.shape[2], queries.shape[3])
    score_sum = jnp.zeros((query_rows.shape[1], train_grads.shape[1]), jnp.float32)
    for layer_index in range(layer_count):
        eigen_row = eigenvalues[layer_index]
        inverse_damped = 1.0 / (eigen_row + 0.1 * jnp.mean(eigen_row))
        train_turned = rotate_rows(train_grads[layer_index], bases[layer_index]).astype(jnp.bfloat16)
        query_turned = (rotate_rows(query_rows[layer_index], bases[layer_index]) * inverse_damped).astype(jnp.bfloat16)
        score_sum = score_sum + jnp.dot(query_turned, train_turned.T, preferred_element_type=jnp.float32)
    return score_sum.reshape(queries.shape[1], queries.shape[2], train_grads.shape[1])
```

```python
import jax
import jax.numpy as jnp
from jax import lax
from jax.sharding import PartitionSpec as P


def spread_queries(queries, full_bases, inverse_damped):
    layer_count, row_count, flat_width = queries.shape
    k = full_bases.shape[1]
    u = full_bases[:, :, :k]
    v = full_bases[:, :, k:]
    square = queries.reshape(layer_count, row_count, k, k)
    f32 = jnp.float32
    half = jnp.einsum("lrab,lbc->lrac", square, v, preferred_element_type=f32).astype(jnp.bfloat16)
    full = jnp.einsum("lca,lrcb->lrab", u, half, preferred_element_type=f32)
    scaled = (full * inverse_damped.reshape(layer_count, 1, k, k)).astype(jnp.bfloat16)
    back = jnp.einsum("lca,lrab->lrcb", u, scaled, preferred_element_type=f32).astype(jnp.bfloat16)
    out = jnp.einsum("lrac,lbc->lrab", back, v, preferred_element_type=f32).astype(jnp.bfloat16)
    return out.reshape(layer_count, row_count, flat_width)


def body(train_grads, queries, bases, eigenvalues):
    full_bases = lax.all_gather(bases, ("blk", "rep"), axis=1, tiled=True)
    eigen_full = lax.all_gather(eigenvalues, ("blk", "rep"), axis=1, tiled=True)
    inverse_damped = 1.0 / (eigen_full + 0.1 * jnp.mean(eigen_full, axis=1, keepdims=True))
    ready = spread_queries(queries[:, 0], full_bases, inverse_damped)
    ready = lax.all_gather(ready, "blk", axis=1, tiled=True)
    partial_scores = jnp.einsum(
        "lqp,ltp->qt", ready, train_grads, preferred_element_type=jnp.float32
    )
    owned = lax.psum_scatter(partial_scores, "layer", scatter_dimension=0, tiled=True)
    return owned[None]


def solution(mesh):
    return jax.shard_map(
        body,
        mesh=mesh,
        in_specs=(
            P("layer", ("groups", "blk"), None),
            P("layer", "rep", ("groups", "blk"), None),
            P("layer", ("blk", "rep"), None),
            P("layer", ("blk", "rep")),
        ),
        out_specs=P("rep", "layer", ("groups", "blk")),
        check_vma=False,
    )
```

```python
import functools
import jax
import jax.numpy as jnp
from jax import lax
from jax.experimental import pallas as pl
from jax.experimental.pallas import tpu as pltpu
from jax.sharding import PartitionSpec as P

MESH = pl.DeviceIdType.MESH
F32 = jnp.float32
BF16 = jnp.bfloat16
LANES = 128
CHUNKS = 4


def mm(a, b):
    return jnp.dot(a, b, preferred_element_type=F32)


def mm_t(a, b):
    return lax.dot_general(a, b, (((1,), (1,)), ((), ())), preferred_element_type=F32)


def one_hot(cond):
    return jnp.where(cond, 1.0, 0.0).astype(BF16)


def iota(shape, dim):
    return lax.broadcasted_iota(jnp.int32, shape, dim)


def kernel(
    n_blk, n_rep, n_layer,
    train_hbm, query_hbm, bases_ref, eigen_ref, out_ref,
    train, query, packet, packets, basis, eigen, square, gathered, total, sent, got,
    train_sem, query_sem, pack_send, pack_recv,
    up_send, up_recv, down_send, down_recv, ex_send, ex_recv,
):
    z = lax.axis_index("blk")
    rep = lax.axis_index("rep")
    layer = lax.axis_index("layer")
    n_peer = n_blk * n_rep
    me = z * n_rep + rep
    basis_rows = bases_ref.shape[1]
    eigen_rows = eigen_ref.shape[1] // LANES
    rows, flat = query.shape
    k = basis.shape[0]
    cols = flat // CHUNKS
    seqs = train.shape[1]
    share = n_blk // n_layer
    pairs = flat // LANES
    width = 2 * LANES

    query_copy = pltpu.make_async_copy(query_hbm.at[0, 0], query, query_sem)
    query_copy.start()
    train_copies = [
        pltpu.make_async_copy(
            train_hbm.at[0, :, pl.ds(c * cols, cols)], train.at[c], train_sem.at[c]
        )
        for c in range(CHUNKS)
    ]
    for copy in train_copies:
        copy.start()

    barrier = pltpu.get_barrier_semaphore()
    peers = []
    for d in range(1, n_peer):
        peer = lax.rem(me + d, n_peer)
        peers.append({"blk": peer // n_rep, "rep": lax.rem(peer, n_rep)})
    for peer in peers:
        pl.semaphore_signal(barrier, inc=1, device_id=peer, device_id_type=MESH)
    for d in range(1, n_layer):
        pl.semaphore_signal(
            barrier, inc=1, device_id={"layer": lax.rem(layer + d, n_layer)}, device_id_type=MESH
        )

    packet[...] = jnp.zeros_like(packet)
    packet[0:basis_rows, :] = bases_ref[0].astype(F32)
    for j in range(eigen_rows):
        packet[basis_rows + j:basis_rows + j + 1, :] = eigen_ref[:, j * LANES:(j + 1) * LANES]
    pl.semaphore_wait(barrier, n_peer - 1 + n_layer - 1)

    pack_copies = []
    for d in range(1, n_peer):
        copy = pltpu.make_async_remote_copy(
            src_ref=packet, dst_ref=packets.at[me],
            send_sem=pack_send.at[d], recv_sem=pack_recv.at[d],
            device_id=peers[d - 1], device_id_type=MESH,
        )
        copy.start()
        pack_copies.append(copy)
    packets[me] = packet[...]
    total[...] = jnp.zeros_like(total)

    wide_row, wide_col = iota((width, width), 0), iota((width, width), 1)
    row_k, col_k = iota((width, k), 0), iota((width, k), 1)
    pick_u = one_hot(col_k == 2 * (row_k & (pairs - 1)) + row_k // LANES)
    pick_v = one_hot(col_k == (row_k & (k - 1)))
    same_u = (wide_row & (LANES - 1)) // pairs == (wide_col & (LANES - 1)) // pairs
    same_v = wide_row // k == wide_col // k

    for copy in pack_copies:
        copy.wait_recv()
    for i in range(n_peer):
        basis[i * basis_rows:(i + 1) * basis_rows, :] = packets[i, 0:basis_rows, :]
        eigen[i * eigen_rows:(i + 1) * eigen_rows, :] = packets[
            i, basis_rows:basis_rows + eigen_rows, :
        ]

    u = basis[:, 0:k].astype(BF16)
    v = basis[:, k:2 * k].astype(BF16)

    def spread(pick, left, same):
        return jnp.where(same, mm_t(left, pick), 0.0).astype(BF16)

    u_turn = spread(pick_u, mm(pick_u, u).astype(BF16), same_u)
    u_back = spread(pick_u, mm_t(pick_u, u).astype(BF16), same_u)
    v_turn = spread(pick_v, mm(pick_v, v).astype(BF16), same_v)
    v_back = spread(pick_v, mm_t(pick_v, v).astype(BF16), same_v)

    eig = eigen[...]
    inverse = 1.0 / (eig + 0.1 * (jnp.sum(eig) / flat))
    group = LANES // pairs
    inverse_t = jnp.concatenate([inverse] * group, axis=0).T
    inverse_t = jnp.concatenate([inverse_t[0:k], inverse_t[k:2 * k]], axis=1)
    batch = 4
    inverse_t = jnp.concatenate([inverse_t] * batch, axis=0)

    query_copy.wait()
    for c in range(flat // width):
        half = mm(query[:, c * width:(c + 1) * width], v_turn).astype(BF16).astype(F32)
        for j in range(2):
            square[pl.ds(2 * c + j, rows, stride=pairs), :] = half[:, j * LANES:(j + 1) * LANES]
    for b in range(rows // group // batch):
        stack = []
        for g in range(batch):
            at = (b * batch + g) * LANES
            t = square[at:at + LANES, :].T
            stack.append(jnp.concatenate([t[0:k], t[k:2 * k]], axis=1))
        a = jnp.concatenate(stack, axis=0).astype(BF16)
        scaled = (mm(a, u_turn) * inverse_t).astype(BF16)
        back = mm(scaled, u_back)
        for g in range(batch):
            at = (b * batch + g) * LANES
            part = back[g * k:(g + 1) * k]
            square[at:at + LANES, :] = jnp.concatenate(
                [part[:, 0:LANES], part[:, LANES:width]], axis=0
            ).T

    def up_copy(s, c):
        return pltpu.make_async_remote_copy(
            src_ref=gathered.at[s, c], dst_ref=gathered.at[s, c],
            send_sem=up_send.at[s, c], recv_sem=up_recv.at[s, c],
            device_id={"blk": lax.rem(z + 1, n_blk)}, device_id_type=MESH,
        )

    def down_copy(s, c):
        return pltpu.make_async_remote_copy(
            src_ref=gathered.at[s, c], dst_ref=gathered.at[s, c],
            send_sem=down_send.at[s, c], recv_sem=down_recv.at[s, c],
            device_id={"blk": lax.rem(z + n_blk - 1, n_blk)}, device_id_type=MESH,
        )

    per_chunk = cols // width
    for c in range(flat // width):
        x = jnp.concatenate(
            [square[pl.ds(2 * c + j, rows, stride=pairs), :] for j in range(2)], axis=1
        ).astype(BF16)
        at = (c % per_chunk) * width
        gathered[z, c // per_chunk, :, at:at + width] = mm(x, v_back).astype(BF16)
        if c % per_chunk == per_chunk - 1:
            done = c // per_chunk

            @pl.when(z > 0)
            def _():
                down_copy(z, done).start()

            @pl.when(z < n_blk - 1)
            def _():
                up_copy(z, done).start()

    def score(s, c):
        x = gathered[s, c]
        tile = 256

        def one(t, carry):
            at = pl.ds(pl.multiple_of(t * tile, tile), tile)
            total[s, :, at] += mm_t(x, train[c, at, :])
            return carry

        lax.fori_loop(0, seqs // tile, one, 0)

    def ex_copy(s):
        owner = s // share
        return pltpu.make_async_remote_copy(
            src_ref=sent.at[s], dst_ref=got.at[layer, lax.rem(s, share)],
            send_sem=ex_send.at[s], recv_sem=ex_recv.at[layer, lax.rem(s, share)],
            device_id={"layer": owner}, device_id_type=MESH,
        )

    def finish(s):
        @pl.when(s // share != layer)
        def _():
            sent[s] = total[s].astype(BF16)
            ex_copy(s).start()

    for copy in train_copies:
        copy.wait()

    def own(c, carry):
        score(z, c)
        return carry

    lax.fori_loop(0, CHUNKS, own, 0)
    finish(z)

    def step(i, carry):
        far = 1 + i // CHUNKS
        c = lax.rem(i, CHUNKS)
        above, below = z + far, z - far

        @pl.when(above < n_blk)
        def _():
            down_copy(above, c).wait_recv()

            @pl.when(z > 0)
            def _():
                down_copy(above, c).start()

        @pl.when(below >= 0)
        def _():
            up_copy(below, c).wait_recv()

            @pl.when(z < n_blk - 1)
            def _():
                up_copy(below, c).start()

        @pl.when(above < n_blk)
        def _():
            score(above, c)

            @pl.when(c == CHUNKS - 1)
            def _():
                finish(above)

        @pl.when(below >= 0)
        def _():
            score(below, c)

            @pl.when(c == CHUNKS - 1)
            def _():
                finish(below)

        return carry

    lax.fori_loop(0, (n_blk - 1) * CHUNKS, step, 0)

    for at in range(share):
        mine = layer * share + at
        for other in range(n_layer):
            @pl.when(layer != other)
            def _():
                pltpu.make_async_remote_copy(
                    src_ref=sent.at[0], dst_ref=got.at[other, at],
                    send_sem=ex_send.at[0], recv_sem=ex_recv.at[other, at],
                    device_id={"layer": other}, device_id_type=MESH,
                ).wait_recv()
                total[mine] += got[other, at].astype(F32)
        out_ref[at * rows:(at + 1) * rows, :] = total[mine]

    for copy in pack_copies:
        copy.wait_send()

    def drain(i, carry):
        s, c = i // CHUNKS, lax.rem(i, CHUNKS)

        @pl.when((s >= z) & (z > 0))
        def _():
            down_copy(s, c).wait_send()

        @pl.when((s <= z) & (z < n_blk - 1))
        def _():
            up_copy(s, c).wait_send()

        @pl.when((c == 0) & (s // share != layer))
        def _():
            ex_copy(s).wait_send()

        return carry

    lax.fori_loop(0, n_blk * CHUNKS, drain, 0)


def body(n_blk, n_rep, n_layer, train_grads, queries, bases, eigenvalues):
    seqs, flat = train_grads.shape[1:]
    rows = queries.shape[2]
    k = bases.shape[2] // 2
    n_peer = n_blk * n_rep
    packet_rows = -(-(bases.shape[1] + eigenvalues.shape[1] // LANES) // 8) * 8
    share = n_blk // n_layer
    cols = flat // CHUNKS
    vmem = pl.BlockSpec(memory_space=pltpu.VMEM)
    hbm = pl.BlockSpec(memory_space=pl.ANY)
    dma = pltpu.SemaphoreType.DMA
    out = pl.pallas_call(
        functools.partial(kernel, n_blk, n_rep, n_layer),
        out_shape=jax.ShapeDtypeStruct((share * rows, seqs), F32),
        in_specs=[hbm, hbm, vmem, vmem],
        out_specs=vmem,
        scratch_shapes=[
            pltpu.VMEM((CHUNKS, seqs, cols), BF16),
            pltpu.VMEM((rows, flat), BF16),
            pltpu.VMEM((packet_rows, LANES), F32),
            pltpu.VMEM((n_peer, packet_rows, LANES), F32),
            pltpu.VMEM((k, 2 * k), F32),
            pltpu.VMEM((flat // LANES, LANES), F32),
            pltpu.VMEM((rows * flat // LANES, LANES), F32),
            pltpu.VMEM((n_blk, CHUNKS, rows, cols), BF16),
            pltpu.VMEM((n_blk, rows, seqs), F32),
            pltpu.VMEM((n_blk, rows, seqs), BF16),
            pltpu.VMEM((n_layer, share, rows, seqs), BF16),
            dma((CHUNKS,)),
            dma,
            dma((n_peer,)),
            dma((n_peer,)),
            dma((n_blk, CHUNKS)),
            dma((n_blk, CHUNKS)),
            dma((n_blk, CHUNKS)),
            dma((n_blk, CHUNKS)),
            dma((n_blk,)),
            dma((n_layer, share)),
        ],
        compiler_params=pltpu.CompilerParams(
            collective_id=0, has_side_effects=True, vmem_limit_bytes=52 * 2**20
        ),
        name="influence",
    )(train_grads, queries, bases, eigenvalues)
    return out[None]


def solution(mesh):
    sizes = mesh.shape
    return jax.shard_map(
        functools.partial(body, sizes["blk"], sizes["rep"], sizes["layer"]),
        mesh=mesh,
        in_specs=(
            P("layer", ("groups", "blk"), None),
            P("layer", "rep", ("groups", "blk"), None),
            P("layer", ("blk", "rep"), None),
            P("layer", ("blk", "rep")),
        ),
        out_specs=P("rep", "layer", ("groups", "blk")),
        check_vma=False,
    )
```

```python
import functools
import jax
import jax.numpy as jnp
from jax import lax
from jax.experimental import pallas as pl
from jax.experimental.pallas import tpu as pltpu
from jax.sharding import PartitionSpec as P

MESH = pl.DeviceIdType.MESH
F32 = jnp.float32
BF16 = jnp.bfloat16
LANES = 128
CHUNKS = 4
TILE = 256


def mm(a, b):
    return jnp.dot(a, b, preferred_element_type=F32)


def mm_t(a, b):
    return lax.dot_general(a, b, (((1,), (1,)), ((), ())), preferred_element_type=F32)


def one_hot(cond):
    return jnp.where(cond, 1.0, 0.0).astype(BF16)


def iota(shape, dim):
    return lax.broadcasted_iota(jnp.int32, shape, dim)


def kernel(
    n_blk, n_rep, n_layer,
    train_hbm, query_hbm, bases_hbm, eigen_hbm, out_ref,
    bases_ref, eigen_ref, train, query, raw, packet, packets, basis, eigen, square, gathered,
    total, sent, got,
    train_sem, query_sem, bases_sem, eigen_sem, pack_send, pack_recv, raw_send, raw_recv,
    up_send, up_recv, down_send, down_recv, ex_send, ex_recv,
):
    z = lax.axis_index("blk")
    rep = lax.axis_index("rep")
    layer = lax.axis_index("layer")
    n_peer = n_blk * n_rep
    me = z * n_rep + rep
    basis_rows = bases_ref.shape[0]
    eigen_rows = eigen_ref.shape[1] // LANES
    rows, flat = query.shape
    k = basis.shape[0]
    cols = flat // CHUNKS
    seqs = train.shape[1]
    share = n_blk // n_layer
    pairs = flat // LANES
    width = 2 * LANES

    bases_copy = pltpu.make_async_copy(bases_hbm.at[0], bases_ref, bases_sem)
    bases_copy.start()
    eigen_copy = pltpu.make_async_copy(eigen_hbm, eigen_ref, eigen_sem)
    eigen_copy.start()
    query_copy = pltpu.make_async_copy(query_hbm.at[0, 0], query, query_sem)
    query_copy.start()
    train_copies = [
        pltpu.make_async_copy(
            train_hbm.at[0, :, pl.ds(c * cols, cols)], train.at[c], train_sem.at[c]
        )
        for c in range(CHUNKS)
    ]

    barrier = pltpu.get_barrier_semaphore()
    peers = []
    for d in range(1, n_peer):
        peer = lax.rem(me + d, n_peer)
        peers.append({"blk": peer // n_rep, "rep": lax.rem(peer, n_rep)})
    for peer in peers:
        pl.semaphore_signal(barrier, inc=1, device_id=peer, device_id_type=MESH)
    for d in range(1, n_layer):
        pl.semaphore_signal(
            barrier, inc=1, device_id={"layer": lax.rem(layer + d, n_layer)}, device_id_type=MESH
        )

    packet[...] = jnp.zeros_like(packet)
    bases_copy.wait()
    eigen_copy.wait()
    packet[0:basis_rows, :] = bases_ref[...].astype(F32)
    for j in range(eigen_rows):
        packet[basis_rows + j:basis_rows + j + 1, :] = eigen_ref[:, j * LANES:(j + 1) * LANES]
    pl.semaphore_wait(barrier, n_peer - 1 + n_layer - 1)

    pack_copies = []
    for d in range(1, n_peer):
        copy = pltpu.make_async_remote_copy(
            src_ref=packet, dst_ref=packets.at[me],
            send_sem=pack_send.at[d], recv_sem=pack_recv.at[d],
            device_id=peers[d - 1], device_id_type=MESH,
        )
        copy.start()
        pack_copies.append(copy)
    packets[me] = packet[...]

    def raw_copy(side, to):
        return pltpu.make_async_remote_copy(
            src_ref=query_hbm.at[0, 0], dst_ref=raw,
            send_sem=raw_send.at[side], recv_sem=raw_recv,
            device_id={"blk": to}, device_id_type=MESH,
        )

    down_raw = raw_copy(0, lax.rem(z + n_blk - 1, n_blk))
    up_raw = raw_copy(1, lax.rem(z + 1, n_blk))

    @pl.when(z == 1)
    def _():
        down_raw.start()

    @pl.when(z == n_blk - 2)
    def _():
        up_raw.start()

    for copy in train_copies:
        copy.start()
    total[...] = jnp.zeros_like(total)

    wide_row, wide_col = iota((width, width), 0), iota((width, width), 1)
    row_k, col_k = iota((width, k), 0), iota((width, k), 1)
    pick_u = one_hot(col_k == 2 * (row_k & (pairs - 1)) + row_k // LANES)
    pick_v = one_hot(col_k == (row_k & (k - 1)))
    same_u = (wide_row & (LANES - 1)) // pairs == (wide_col & (LANES - 1)) // pairs
    same_v = wide_row // k == wide_col // k

    for copy in pack_copies:
        copy.wait_recv()
    for i in range(n_peer):
        basis[i * basis_rows:(i + 1) * basis_rows, :] = packets[i, 0:basis_rows, :]
        eigen[i * eigen_rows:(i + 1) * eigen_rows, :] = packets[
            i, basis_rows:basis_rows + eigen_rows, :
        ]

    u = basis[:, 0:k].astype(BF16)
    v = basis[:, k:2 * k].astype(BF16)

    def spread(pick, left, same):
        return jnp.where(same, mm_t(left, pick), 0.0).astype(BF16)

    u_turn = spread(pick_u, mm(pick_u, u).astype(BF16), same_u)
    u_back = spread(pick_u, mm_t(pick_u, u).astype(BF16), same_u)
    v_turn = spread(pick_v, mm(pick_v, v).astype(BF16), same_v)
    v_back = spread(pick_v, mm_t(pick_v, v).astype(BF16), same_v)

    eig = eigen[...]
    inverse = 1.0 / (eig + 0.1 * (jnp.sum(eig) / flat))
    group = LANES // pairs
    inverse_t = jnp.concatenate([inverse] * group, axis=0).T
    inverse_t = jnp.concatenate([inverse_t[0:k], inverse_t[k:2 * k]], axis=1)
    batch = 4
    inverse_t = jnp.concatenate([inverse_t] * batch, axis=0)

    def up_copy(s, c):
        return pltpu.make_async_remote_copy(
            src_ref=gathered.at[s, c], dst_ref=gathered.at[s, c],
            send_sem=up_send.at[s, c], recv_sem=up_recv.at[s, c],
            device_id={"blk": lax.rem(z + 1, n_blk)}, device_id_type=MESH,
        )

    def down_copy(s, c):
        return pltpu.make_async_remote_copy(
            src_ref=gathered.at[s, c], dst_ref=gathered.at[s, c],
            send_sem=down_send.at[s, c], recv_sem=down_recv.at[s, c],
            device_id={"blk": lax.rem(z + n_blk - 1, n_blk)}, device_id_type=MESH,
        )

    def turn(source, s, on_chunk):
        for c in range(flat // width):
            half = mm(source[:, c * width:(c + 1) * width], v_turn).astype(BF16).astype(F32)
            for j in range(2):
                square[pl.ds(2 * c + j, rows, stride=pairs), :] = half[:, j * LANES:(j + 1) * LANES]
        for b in range(rows // group // batch):
            stack = []
            for g in range(batch):
                at = (b * batch + g) * LANES
                t = square[at:at + LANES, :].T
                stack.append(jnp.concatenate([t[0:k], t[k:2 * k]], axis=1))
            a = jnp.concatenate(stack, axis=0).astype(BF16)
            scaled = (mm(a, u_turn) * inverse_t).astype(BF16)
            back = mm(scaled, u_back)
            for g in range(batch):
                at = (b * batch + g) * LANES
                part = back[g * k:(g + 1) * k]
                square[at:at + LANES, :] = jnp.concatenate(
                    [part[:, 0:LANES], part[:, LANES:width]], axis=0
                ).T
        per_chunk = cols // width
        for c in range(flat // width):
            x = jnp.concatenate(
                [square[pl.ds(2 * c + j, rows, stride=pairs), :] for j in range(2)], axis=1
            ).astype(BF16)
            at = (c % per_chunk) * width
            gathered[s, c // per_chunk, :, at:at + width] = mm(x, v_back).astype(BF16)
            if c % per_chunk == per_chunk - 1:
                on_chunk(c // per_chunk)

    def send_own(c):
        @pl.when(z > 1)
        def _():
            down_copy(z, c).start()

        @pl.when(z < n_blk - 2)
        def _():
            up_copy(z, c).start()

    query_copy.wait()
    turn(query, z, send_own)

    def ex_copy(s, t):
        return pltpu.make_async_remote_copy(
            src_ref=sent.at[s, t], dst_ref=got.at[layer, lax.rem(s, share), t],
            send_sem=ex_send.at[s, t], recv_sem=ex_recv.at[layer, lax.rem(s, share), t],
            device_id={"layer": s // share}, device_id_type=MESH,
        )

    def score(s, c):
        x = gathered[s, c]

        def one(t, carry):
            at = pl.ds(pl.multiple_of(t * TILE, TILE), TILE)
            total[s, :, at] += mm_t(x, train[c, at, :])

            @pl.when((c == CHUNKS - 1) & (s // share != layer))
            def _():
                sent[s, t] = total[s, :, at].astype(BF16)
                ex_copy(s, t).start()

            return carry

        lax.fori_loop(0, seqs // TILE, one, 0)

    for copy in train_copies:
        copy.wait()

    def own(c, carry):
        score(z, c)
        return carry

    lax.fori_loop(0, CHUNKS, own, 0)

    if n_blk > 1:
        @pl.when((z == 0) | (z == n_blk - 1))
        def _():
            near = 1 + (z // (n_blk - 1)) * (n_blk - 3)
            down_raw.wait_recv()
            turn(raw, near, lambda c: None)

            def close(c, carry):
                score(near, c)
                return carry

            lax.fori_loop(0, CHUNKS, close, 0)

    def step(i, carry):
        far = 1 + i // CHUNKS
        c = lax.rem(i, CHUNKS)
        above, below = z + far, z - far
        from_above = (above < n_blk) & (z + far > 1)
        from_below = (below >= 0) & (n_blk - 1 - z + far > 1)

        @pl.when(from_above)
        def _():
            down_copy(above, c).wait_recv()

            @pl.when(z > 0)
            def _():
                down_copy(above, c).start()

        @pl.when(from_below)
        def _():
            up_copy(below, c).wait_recv()

            @pl.when(z < n_blk - 1)
            def _():
                up_copy(below, c).start()

        @pl.when(from_above)
        def _():
            score(above, c)

        @pl.when(from_below)
        def _():
            score(below, c)

        return carry

    lax.fori_loop(0, (n_blk - 1) * CHUNKS, step, 0)

    tiles = seqs // TILE
    high = (2 * z) // n_blk

    def collect(i, carry):
        at, t = i // tiles, lax.rem(i, tiles)
        at = at + high * (share - 1 - 2 * at)
        span = pl.ds(pl.multiple_of(t * TILE, TILE), TILE)
        mine = layer * share + at
        for other in range(n_layer):
            @pl.when(layer != other)
            def _():
                pltpu.make_async_remote_copy(
                    src_ref=sent.at[0, 0], dst_ref=got.at[other, at, t],
                    send_sem=ex_send.at[0, 0], recv_sem=ex_recv.at[other, at, t],
                    device_id={"layer": other}, device_id_type=MESH,
                ).wait_recv()
                total[mine, :, span] += got[other, at, t].astype(F32)
        out_ref[pl.ds(pl.multiple_of(at * rows, rows), rows), span] = total[mine, :, span]
        return carry

    lax.fori_loop(0, share * tiles, collect, 0)

    for copy in pack_copies:
        copy.wait_send()

    @pl.when(z == 1)
    def _():
        down_raw.wait_send()

    @pl.when(z == n_blk - 2)
    def _():
        up_raw.wait_send()

    def drain(i, carry):
        s, c = i // CHUNKS, lax.rem(i, CHUNKS)

        @pl.when((s >= z) & (z > 0) & (s + z > 2))
        def _():
            down_copy(s, c).wait_send()

        @pl.when((s <= z) & (z < n_blk - 1) & (2 * (n_blk - 1) - s - z > 2))
        def _():
            up_copy(s, c).wait_send()

        return carry

    lax.fori_loop(0, n_blk * CHUNKS, drain, 0)

    def drain_ex(i, carry):
        s, t = i // tiles, lax.rem(i, tiles)

        @pl.when(s // share != layer)
        def _():
            ex_copy(s, t).wait_send()

        return carry

    lax.fori_loop(0, n_blk * tiles, drain_ex, 0)


def body(n_blk, n_rep, n_layer, train_grads, queries, bases, eigenvalues):
    seqs, flat = train_grads.shape[1:]
    rows = queries.shape[2]
    k = bases.shape[2] // 2
    n_peer = n_blk * n_rep
    packet_rows = -(-(bases.shape[1] + eigenvalues.shape[1] // LANES) // 8) * 8
    share = n_blk // n_layer
    cols = flat // CHUNKS
    tiles = seqs // TILE
    vmem = pl.BlockSpec(memory_space=pltpu.VMEM)
    hbm = pl.BlockSpec(memory_space=pltpu.HBM)
    dma = pltpu.SemaphoreType.DMA
    out = pl.pallas_call(
        functools.partial(kernel, n_blk, n_rep, n_layer),
        out_shape=jax.ShapeDtypeStruct((share * rows, seqs), F32),
        in_specs=[hbm] * 4,
        out_specs=vmem,
        scratch_shapes=[
            pltpu.VMEM(bases.shape[1:], BF16),
            pltpu.VMEM(eigenvalues.shape, F32),
            pltpu.VMEM((CHUNKS, seqs, cols), BF16),
            pltpu.VMEM((rows, flat), BF16),
            pltpu.VMEM((rows, flat), BF16),
            pltpu.VMEM((packet_rows, LANES), F32),
            pltpu.VMEM((n_peer, packet_rows, LANES), F32),
            pltpu.VMEM((k, 2 * k), F32),
            pltpu.VMEM((flat // LANES, LANES), F32),
            pltpu.VMEM((rows * flat // LANES, LANES), F32),
            pltpu.VMEM((n_blk, CHUNKS, rows, cols), BF16),
            pltpu.VMEM((n_blk, rows, seqs), F32),
            pltpu.VMEM((n_blk, tiles, rows, TILE), BF16),
            pltpu.VMEM((n_layer, share, tiles, rows, TILE), BF16),
            dma((CHUNKS,)),
            dma,
            dma,
            dma,
            dma((n_peer,)),
            dma((n_peer,)),
            dma((2,)),
            dma,
            dma((n_blk, CHUNKS)),
            dma((n_blk, CHUNKS)),
            dma((n_blk, CHUNKS)),
            dma((n_blk, CHUNKS)),
            dma((n_blk, tiles)),
            dma((n_layer, share, tiles)),
        ],
        compiler_params=pltpu.CompilerParams(
            collective_id=0, has_side_effects=True, vmem_limit_bytes=52 * 2**20
        ),
        name="influence",
    )(train_grads, queries, bases, eigenvalues)
    return out[None]


def solution(mesh):
    sizes = mesh.shape
    return jax.shard_map(
        functools.partial(body, sizes["blk"], sizes["rep"], sizes["layer"]),
        mesh=mesh,
        in_specs=(
            P("layer", ("groups", "blk"), None),
            P("layer", "rep", ("groups", "blk"), None),
            P("layer", ("blk", "rep"), None),
            P("layer", ("blk", "rep")),
        ),
        out_specs=P("rep", "layer", ("groups", "blk")),
        check_vma=False,
    )
```

```python
import functools
import jax
import jax.numpy as jnp
from jax import lax
from jax.experimental import pallas as pl
from jax.experimental.pallas import tpu as pltpu
from jax.sharding import PartitionSpec as P

MESH = pl.DeviceIdType.MESH
F32 = jnp.float32
BF16 = jnp.bfloat16
LANES = 128
CHUNKS = 4
TILE = 256


def mm(a, b):
    return jnp.dot(a, b, preferred_element_type=F32)


def mm_t(a, b):
    return lax.dot_general(a, b, (((1,), (1,)), ((), ())), preferred_element_type=F32)


def one_hot(cond):
    return jnp.where(cond, 1.0, 0.0).astype(BF16)


def iota(shape, dim):
    return lax.broadcasted_iota(jnp.int32, shape, dim)


def kernel(
    n_blk, n_rep, n_layer,
    train_hbm, query_hbm, bases_hbm, eigen_hbm, out_hbm,
    bases_ref, eigen_ref, train, query, raw, packet, packets, basis, eigen, square, gathered,
    total, sent, got,
    train_sem, query_sem, bases_sem, eigen_sem, pack_send, pack_recv, raw_send, raw_recv,
    up_send, up_recv, down_send, down_recv, ex_send, ex_recv, out_sem,
):
    z = lax.axis_index("blk")
    rep = lax.axis_index("rep")
    layer = lax.axis_index("layer")
    n_peer = n_blk * n_rep
    me = z * n_rep + rep
    basis_rows = bases_ref.shape[0]
    eigen_rows = eigen_ref.shape[1] // LANES
    rows, flat = query.shape
    k = basis.shape[0]
    cols = flat // CHUNKS
    seqs = train.shape[1]
    share = n_blk // n_layer
    pairs = flat // LANES
    width = 2 * LANES

    bases_copy = pltpu.make_async_copy(bases_hbm.at[0], bases_ref, bases_sem)
    bases_copy.start()
    eigen_copy = pltpu.make_async_copy(eigen_hbm, eigen_ref, eigen_sem)
    eigen_copy.start()
    query_copy = pltpu.make_async_copy(query_hbm.at[0, 0], query, query_sem)
    query_copy.start()
    train_copies = [
        pltpu.make_async_copy(
            train_hbm.at[0, :, pl.ds(c * cols, cols)], train.at[c], train_sem.at[c]
        )
        for c in range(CHUNKS)
    ]

    barrier = pltpu.get_barrier_semaphore()
    peers = []
    for d in range(1, n_peer):
        peer = lax.rem(me + d, n_peer)
        peers.append({"blk": peer // n_rep, "rep": lax.rem(peer, n_rep)})
    for peer in peers:
        pl.semaphore_signal(barrier, inc=1, device_id=peer, device_id_type=MESH)
    for d in range(1, n_layer):
        pl.semaphore_signal(
            barrier, inc=1, device_id={"layer": lax.rem(layer + d, n_layer)}, device_id_type=MESH
        )

    packet[...] = jnp.zeros_like(packet)
    bases_copy.wait()
    eigen_copy.wait()
    packet[0:basis_rows, :] = bases_ref[...].astype(F32)
    for j in range(eigen_rows):
        packet[basis_rows + j:basis_rows + j + 1, :] = eigen_ref[:, j * LANES:(j + 1) * LANES]
    pl.semaphore_wait(barrier, n_peer - 1 + n_layer - 1)

    pack_copies = []
    for d in range(1, n_peer):
        copy = pltpu.make_async_remote_copy(
            src_ref=packet, dst_ref=packets.at[me],
            send_sem=pack_send.at[d], recv_sem=pack_recv.at[d],
            device_id=peers[d - 1], device_id_type=MESH,
        )
        copy.start()
        pack_copies.append(copy)
    packets[me] = packet[...]

    def raw_copy(side, to):
        return pltpu.make_async_remote_copy(
            src_ref=query_hbm.at[0, 0], dst_ref=raw,
            send_sem=raw_send.at[side], recv_sem=raw_recv,
            device_id={"blk": to}, device_id_type=MESH,
        )

    down_raw = raw_copy(0, lax.rem(z + n_blk - 1, n_blk))
    up_raw = raw_copy(1, lax.rem(z + 1, n_blk))

    @pl.when(z == 1)
    def _():
        down_raw.start()

    @pl.when(z == n_blk - 2)
    def _():
        up_raw.start()

    for copy in train_copies:
        copy.start()
    total[...] = jnp.zeros_like(total)

    wide_row, wide_col = iota((width, width), 0), iota((width, width), 1)
    row_k, col_k = iota((width, k), 0), iota((width, k), 1)
    pick_u = one_hot(col_k == 2 * (row_k & (pairs - 1)) + row_k // LANES)
    pick_v = one_hot(col_k == (row_k & (k - 1)))
    same_u = (wide_row & (LANES - 1)) // pairs == (wide_col & (LANES - 1)) // pairs
    same_v = wide_row // k == wide_col // k

    for copy in pack_copies:
        copy.wait_recv()
    for i in range(n_peer):
        basis[i * basis_rows:(i + 1) * basis_rows, :] = packets[i, 0:basis_rows, :]
        eigen[i * eigen_rows:(i + 1) * eigen_rows, :] = packets[
            i, basis_rows:basis_rows + eigen_rows, :
        ]

    u = basis[:, 0:k].astype(BF16)
    v = basis[:, k:2 * k].astype(BF16)

    def spread(pick, left, same):
        return jnp.where(same, mm_t(left, pick), 0.0).astype(BF16)

    u_turn = spread(pick_u, mm(pick_u, u).astype(BF16), same_u)
    u_back = spread(pick_u, mm_t(pick_u, u).astype(BF16), same_u)
    v_turn = spread(pick_v, mm(pick_v, v).astype(BF16), same_v)
    v_back = spread(pick_v, mm_t(pick_v, v).astype(BF16), same_v)

    eig = eigen[...]
    inverse = 1.0 / (eig + 0.1 * (jnp.sum(eig) / flat))
    group = LANES // pairs
    inverse_t = jnp.concatenate([inverse] * group, axis=0).T
    inverse_t = jnp.concatenate([inverse_t[0:k], inverse_t[k:2 * k]], axis=1)
    batch = 4
    inverse_t = jnp.concatenate([inverse_t] * batch, axis=0)

    def up_copy(s, c):
        return pltpu.make_async_remote_copy(
            src_ref=gathered.at[s, c], dst_ref=gathered.at[s, c],
            send_sem=up_send.at[s, c], recv_sem=up_recv.at[s, c],
            device_id={"blk": lax.rem(z + 1, n_blk)}, device_id_type=MESH,
        )

    def down_copy(s, c):
        return pltpu.make_async_remote_copy(
            src_ref=gathered.at[s, c], dst_ref=gathered.at[s, c],
            send_sem=down_send.at[s, c], recv_sem=down_recv.at[s, c],
            device_id={"blk": lax.rem(z + n_blk - 1, n_blk)}, device_id_type=MESH,
        )

    def turn(source, s, on_chunk):
        for c in range(flat // width):
            half = mm(source[:, c * width:(c + 1) * width], v_turn).astype(BF16).astype(F32)
            for j in range(2):
                square[pl.ds(2 * c + j, rows, stride=pairs), :] = half[:, j * LANES:(j + 1) * LANES]
        for b in range(rows // group // batch):
            stack = []
            for g in range(batch):
                at = (b * batch + g) * LANES
                t = square[at:at + LANES, :].T
                stack.append(jnp.concatenate([t[0:k], t[k:2 * k]], axis=1))
            a = jnp.concatenate(stack, axis=0).astype(BF16)
            scaled = (mm(a, u_turn) * inverse_t).astype(BF16)
            back = mm(scaled, u_back)
            for g in range(batch):
                at = (b * batch + g) * LANES
                part = back[g * k:(g + 1) * k]
                square[at:at + LANES, :] = jnp.concatenate(
                    [part[:, 0:LANES], part[:, LANES:width]], axis=0
                ).T
        per_chunk = cols // width
        for c in range(flat // width):
            x = jnp.concatenate(
                [square[pl.ds(2 * c + j, rows, stride=pairs), :] for j in range(2)], axis=1
            ).astype(BF16)
            at = (c % per_chunk) * width
            gathered[s, c // per_chunk, :, at:at + width] = mm(x, v_back).astype(BF16)
            if c % per_chunk == per_chunk - 1:
                on_chunk(c // per_chunk)

    def send_own(c):
        @pl.when(z > 1)
        def _():
            down_copy(z, c).start()

        @pl.when(z < n_blk - 2)
        def _():
            up_copy(z, c).start()

    query_copy.wait()
    turn(query, z, send_own)

    def ex_copy(s, t):
        return pltpu.make_async_remote_copy(
            src_ref=sent.at[s, t], dst_ref=got.at[layer, lax.rem(s, share), t],
            send_sem=ex_send.at[s, t], recv_sem=ex_recv.at[layer, lax.rem(s, share), t],
            device_id={"layer": s // share}, device_id_type=MESH,
        )

    def score(shards, c):
        x = jnp.concatenate([gathered[s, c] for s in shards], axis=0)

        def one(t, carry):
            at = pl.ds(pl.multiple_of(t * TILE, TILE), TILE)
            y = mm_t(x, train[c, at, :])
            for j, s in enumerate(shards):
                total[s, :, at] += y[j * rows:(j + 1) * rows]

            @pl.when(c == CHUNKS - 1)
            def _():
                for s in shards:
                    @pl.when(s // share != layer)
                    def _():
                        sent[s, t] = total[s, :, at].astype(BF16)
                        ex_copy(s, t).start()

            return carry

        lax.fori_loop(0, seqs // TILE, one, 0)

    for copy in train_copies:
        copy.wait()

    if n_blk == 1:
        for c in range(CHUNKS):
            score([z], c)

    if n_blk > 1:
        @pl.when((z == 0) | (z == n_blk - 1))
        def _():
            near = 1 + (z // (n_blk - 1)) * (n_blk - 3)
            down_raw.wait_recv()
            turn(raw, near, lambda c: None)

            def close(c, carry):
                score([z, near], c)
                return carry

            lax.fori_loop(0, CHUNKS, close, 0)

    def step(i, carry):
        far = 1 + i // CHUNKS
        c = lax.rem(i, CHUNKS)
        above, below = z + far, z - far
        from_above = (above < n_blk) & (z + far > 1)
        from_below = (below >= 0) & (n_blk - 1 - z + far > 1)

        @pl.when(from_above)
        def _():
            down_copy(above, c).wait_recv()

            @pl.when(z > 0)
            def _():
                down_copy(above, c).start()

        @pl.when(from_below)
        def _():
            up_copy(below, c).wait_recv()

            @pl.when(z < n_blk - 1)
            def _():
                up_copy(below, c).start()

        if n_blk > 2:
            @pl.when((far == 1) & from_above & from_below)
            def _():
                score([z, above, below], c)

        @pl.when(from_above & (far > 1))
        def _():
            score([above], c)

        @pl.when(from_below & (far > 1))
        def _():
            score([below], c)

        return carry

    lax.fori_loop(0, (n_blk - 1) * CHUNKS, step, 0)

    tiles = seqs // TILE
    high = (2 * z) // n_blk

    def out_copy(at, t):
        span = pl.ds(pl.multiple_of(t * TILE, TILE), TILE)
        return pltpu.make_async_copy(
            total.at[layer * share + at, :, span],
            out_hbm.at[pl.ds(pl.multiple_of(at * rows, rows), rows), span],
            out_sem.at[at, t],
        )

    def collect(i, carry):
        at, t = i // tiles, lax.rem(i, tiles)
        at = at + high * (share - 1 - 2 * at)
        span = pl.ds(pl.multiple_of(t * TILE, TILE), TILE)
        mine = layer * share + at
        for other in range(n_layer):
            @pl.when(layer != other)
            def _():
                pltpu.make_async_remote_copy(
                    src_ref=sent.at[0, 0], dst_ref=got.at[other, at, t],
                    send_sem=ex_send.at[0, 0], recv_sem=ex_recv.at[other, at, t],
                    device_id={"layer": other}, device_id_type=MESH,
                ).wait_recv()
                total[mine, :, span] += got[other, at, t].astype(F32)
        out_copy(at, t).start()
        return carry

    lax.fori_loop(0, share * tiles, collect, 0)

    def drain_out(i, carry):
        out_copy(i // tiles, lax.rem(i, tiles)).wait()
        return carry

    lax.fori_loop(0, share * tiles, drain_out, 0)
    for copy in pack_copies:
        copy.wait_send()

    @pl.when(z == 1)
    def _():
        down_raw.wait_send()

    @pl.when(z == n_blk - 2)
    def _():
        up_raw.wait_send()

    def drain(i, carry):
        s, c = i // CHUNKS, lax.rem(i, CHUNKS)

        @pl.when((s >= z) & (z > 0) & (s + z > 2))
        def _():
            down_copy(s, c).wait_send()

        @pl.when((s <= z) & (z < n_blk - 1) & (2 * (n_blk - 1) - s - z > 2))
        def _():
            up_copy(s, c).wait_send()

        return carry

    lax.fori_loop(0, n_blk * CHUNKS, drain, 0)

    def drain_ex(i, carry):
        s, t = i // tiles, lax.rem(i, tiles)

        @pl.when(s // share != layer)
        def _():
            ex_copy(s, t).wait_send()

        return carry

    lax.fori_loop(0, n_blk * tiles, drain_ex, 0)


def body(n_blk, n_rep, n_layer, train_grads, queries, bases, eigenvalues):
    seqs, flat = train_grads.shape[1:]
    rows = queries.shape[2]
    k = bases.shape[2] // 2
    n_peer = n_blk * n_rep
    packet_rows = -(-(bases.shape[1] + eigenvalues.shape[1] // LANES) // 8) * 8
    share = n_blk // n_layer
    cols = flat // CHUNKS
    tiles = seqs // TILE
    hbm = pl.BlockSpec(memory_space=pltpu.HBM)
    dma = pltpu.SemaphoreType.DMA
    out = pl.pallas_call(
        functools.partial(kernel, n_blk, n_rep, n_layer),
        out_shape=jax.ShapeDtypeStruct((share * rows, seqs), F32),
        in_specs=[hbm] * 4,
        out_specs=hbm,
        scratch_shapes=[
            pltpu.VMEM(bases.shape[1:], BF16),
            pltpu.VMEM(eigenvalues.shape, F32),
            pltpu.VMEM((CHUNKS, seqs, cols), BF16),
            pltpu.VMEM((rows, flat), BF16),
            pltpu.VMEM((rows, flat), BF16),
            pltpu.VMEM((packet_rows, LANES), F32),
            pltpu.VMEM((n_peer, packet_rows, LANES), F32),
            pltpu.VMEM((k, 2 * k), F32),
            pltpu.VMEM((flat // LANES, LANES), F32),
            pltpu.VMEM((rows * flat // LANES, LANES), F32),
            pltpu.VMEM((n_blk, CHUNKS, rows, cols), BF16),
            pltpu.VMEM((n_blk, rows, seqs), F32),
            pltpu.VMEM((n_blk, tiles, rows, TILE), BF16),
            pltpu.VMEM((n_layer, share, tiles, rows, TILE), BF16),
            dma((CHUNKS,)),
            dma,
            dma,
            dma,
            dma((n_peer,)),
            dma((n_peer,)),
            dma((2,)),
            dma,
            dma((n_blk, CHUNKS)),
            dma((n_blk, CHUNKS)),
            dma((n_blk, CHUNKS)),
            dma((n_blk, CHUNKS)),
            dma((n_blk, tiles)),
            dma((n_layer, share, tiles)),
            dma((share, tiles)),
        ],
        compiler_params=pltpu.CompilerParams(
            collective_id=0, has_side_effects=True, vmem_limit_bytes=63 * 2**20
        ),
        name="influence",
    )(train_grads, queries, bases, eigenvalues)
    return out[None]


def solution(mesh):
    sizes = mesh.shape
    return jax.shard_map(
        functools.partial(body, sizes["blk"], sizes["rep"], sizes["layer"]),
        mesh=mesh,
        in_specs=(
            P("layer", ("groups", "blk"), None),
            P("layer", "rep", ("groups", "blk"), None),
            P("layer", ("blk", "rep"), None),
            P("layer", ("blk", "rep")),
        ),
        out_specs=P("rep", "layer", ("groups", "blk")),
        check_vma=False,
    )
```

```python
import functools
import jax
import jax.numpy as jnp
from jax import lax
from jax.experimental import pallas as pl
from jax.experimental.pallas import tpu as pltpu
from jax.sharding import PartitionSpec as P

MESH = pl.DeviceIdType.MESH
F32 = jnp.float32
BF16 = jnp.bfloat16
LANES = 128
CHUNKS = 8
TILE = 256


def mm(a, b):
    return jnp.dot(a, b, preferred_element_type=F32)


def mm_t(a, b):
    return lax.dot_general(a, b, (((1,), (1,)), ((), ())), preferred_element_type=F32)


def one_hot(cond):
    return jnp.where(cond, 1.0, 0.0).astype(BF16)


def iota(shape, dim):
    return lax.broadcasted_iota(jnp.int32, shape, dim)


def kernel(
    n_blk, n_rep, n_layer,
    train_hbm, query_hbm, bases_hbm, eigen_hbm, own_hbm, got_hbm,
    bases_ref, eigen_ref, train, query, raw, packet, packets, basis, eigen, square, gathered,
    total, sent,
    train_sem, query_sem, bases_sem, eigen_sem, pack_send, pack_recv, raw_send, raw_recv,
    up_send, up_recv, down_send, down_recv, ex_send, ex_recv, own_sem,
):
    z = lax.axis_index("blk")
    rep = lax.axis_index("rep")
    layer = lax.axis_index("layer")
    n_peer = n_blk * n_rep
    me = z * n_rep + rep
    basis_rows = bases_ref.shape[0]
    eigen_rows = eigen_ref.shape[1] // LANES
    rows, flat = query.shape
    k = basis.shape[0]
    cols = flat // CHUNKS
    seqs = train.shape[1]
    share = n_blk // n_layer
    pairs = flat // LANES
    width = 2 * LANES

    bases_copy = pltpu.make_async_copy(bases_hbm.at[0], bases_ref, bases_sem)
    bases_copy.start()
    eigen_copy = pltpu.make_async_copy(eigen_hbm, eigen_ref, eigen_sem)
    eigen_copy.start()
    query_copy = pltpu.make_async_copy(query_hbm.at[0, 0], query, query_sem)
    query_copy.start()
    train_copies = [
        pltpu.make_async_copy(
            train_hbm.at[0, :, pl.ds(c * cols, cols)], train.at[c], train_sem.at[c]
        )
        for c in range(CHUNKS)
    ]

    barrier = pltpu.get_barrier_semaphore()
    peers = []
    for d in range(1, n_peer):
        peer = lax.rem(me + d, n_peer)
        peers.append({"blk": peer // n_rep, "rep": lax.rem(peer, n_rep)})
    for peer in peers:
        pl.semaphore_signal(barrier, inc=1, device_id=peer, device_id_type=MESH)
    for d in range(1, n_layer):
        pl.semaphore_signal(
            barrier, inc=1, device_id={"layer": lax.rem(layer + d, n_layer)}, device_id_type=MESH
        )

    packet[...] = jnp.zeros_like(packet)
    bases_copy.wait()
    eigen_copy.wait()
    packet[0:basis_rows, :] = bases_ref[...].astype(F32)
    for j in range(eigen_rows):
        packet[basis_rows + j:basis_rows + j + 1, :] = eigen_ref[:, j * LANES:(j + 1) * LANES]
    pl.semaphore_wait(barrier, n_peer - 1 + n_layer - 1)

    pack_copies = []
    for d in range(1, n_peer):
        copy = pltpu.make_async_remote_copy(
            src_ref=packet, dst_ref=packets.at[me],
            send_sem=pack_send.at[d], recv_sem=pack_recv.at[d],
            device_id=peers[d - 1], device_id_type=MESH,
        )
        copy.start()
        pack_copies.append(copy)
    packets[me] = packet[...]

    def raw_copy(side, to):
        return pltpu.make_async_remote_copy(
            src_ref=query_hbm.at[0, 0], dst_ref=raw,
            send_sem=raw_send.at[side], recv_sem=raw_recv,
            device_id={"blk": to}, device_id_type=MESH,
        )

    down_raw = raw_copy(0, lax.rem(z + n_blk - 1, n_blk))
    up_raw = raw_copy(1, lax.rem(z + 1, n_blk))

    @pl.when(z == 1)
    def _():
        down_raw.start()

    @pl.when(z == n_blk - 2)
    def _():
        up_raw.start()

    for copy in train_copies:
        copy.start()
    total[...] = jnp.zeros_like(total)

    wide_row, wide_col = iota((width, width), 0), iota((width, width), 1)
    row_k, col_k = iota((width, k), 0), iota((width, k), 1)
    pick_u = one_hot(col_k == 2 * (row_k & (pairs - 1)) + row_k // LANES)
    pick_v = one_hot(col_k == (row_k & (k - 1)))
    same_u = (wide_row & (LANES - 1)) // pairs == (wide_col & (LANES - 1)) // pairs
    same_v = wide_row // k == wide_col // k

    for copy in pack_copies:
        copy.wait_recv()
    for i in range(n_peer):
        basis[i * basis_rows:(i + 1) * basis_rows, :] = packets[i, 0:basis_rows, :]
        eigen[i * eigen_rows:(i + 1) * eigen_rows, :] = packets[
            i, basis_rows:basis_rows + eigen_rows, :
        ]

    u = basis[:, 0:k].astype(BF16)
    v = basis[:, k:2 * k].astype(BF16)

    def spread(pick, left, same):
        return jnp.where(same, mm_t(left, pick), 0.0).astype(BF16)

    u_turn = spread(pick_u, mm(pick_u, u).astype(BF16), same_u)
    u_back = spread(pick_u, mm_t(pick_u, u).astype(BF16), same_u)
    v_turn = spread(pick_v, mm(pick_v, v).astype(BF16), same_v)
    v_back = spread(pick_v, mm_t(pick_v, v).astype(BF16), same_v)

    eig = eigen[...]
    inverse = 1.0 / (eig + 0.1 * (jnp.sum(eig) / flat))
    group = LANES // pairs
    inverse_t = jnp.concatenate([inverse] * group, axis=0).T
    inverse_t = jnp.concatenate([inverse_t[0:k], inverse_t[k:2 * k]], axis=1)
    batch = 4
    inverse_t = jnp.concatenate([inverse_t] * batch, axis=0)

    def up_copy(s, c):
        return pltpu.make_async_remote_copy(
            src_ref=gathered.at[s, c], dst_ref=gathered.at[s, c],
            send_sem=up_send.at[s, c], recv_sem=up_recv.at[s, c],
            device_id={"blk": lax.rem(z + 1, n_blk)}, device_id_type=MESH,
        )

    def down_copy(s, c):
        return pltpu.make_async_remote_copy(
            src_ref=gathered.at[s, c], dst_ref=gathered.at[s, c],
            send_sem=down_send.at[s, c], recv_sem=down_recv.at[s, c],
            device_id={"blk": lax.rem(z + n_blk - 1, n_blk)}, device_id_type=MESH,
        )

    def turn(source, s, on_chunk):
        for c in range(flat // width):
            half = mm(source[:, c * width:(c + 1) * width], v_turn).astype(BF16).astype(F32)
            for j in range(2):
                square[pl.ds(2 * c + j, rows, stride=pairs), :] = half[:, j * LANES:(j + 1) * LANES]
        for b in range(rows // group // batch):
            stack = []
            for g in range(batch):
                at = (b * batch + g) * LANES
                t = square[at:at + LANES, :].T
                stack.append(jnp.concatenate([t[0:k], t[k:2 * k]], axis=1))
            a = jnp.concatenate(stack, axis=0).astype(BF16)
            scaled = (mm(a, u_turn) * inverse_t).astype(BF16)
            back = mm(scaled, u_back)
            for g in range(batch):
                at = (b * batch + g) * LANES
                part = back[g * k:(g + 1) * k]
                square[at:at + LANES, :] = jnp.concatenate(
                    [part[:, 0:LANES], part[:, LANES:width]], axis=0
                ).T
        per_chunk = cols // width
        for c in range(flat // width):
            x = jnp.concatenate(
                [square[pl.ds(2 * c + j, rows, stride=pairs), :] for j in range(2)], axis=1
            ).astype(BF16)
            at = (c % per_chunk) * width
            gathered[s, c // per_chunk, :, at:at + width] = mm(x, v_back).astype(BF16)
            if c % per_chunk == per_chunk - 1:
                on_chunk(c // per_chunk)

    def send_own(c):
        @pl.when(z > 1)
        def _():
            down_copy(z, c).start()

        @pl.when(z < n_blk - 2)
        def _():
            up_copy(z, c).start()

    query_copy.wait()
    turn(query, z, send_own)

    def place(s, t):
        return (
            pl.ds(pl.multiple_of(lax.rem(s, share) * rows, rows), rows),
            pl.ds(pl.multiple_of(t * TILE, TILE), TILE),
        )

    def ex_copy(s, t):
        slot = lax.rem(layer - s // share + n_layer - 1, n_layer)
        return pltpu.make_async_remote_copy(
            src_ref=sent.at[s, t], dst_ref=got_hbm.at[(slot, *place(s, t))],
            send_sem=ex_send.at[s, t], recv_sem=ex_recv.at[slot, lax.rem(s, share), t],
            device_id={"layer": s // share}, device_id_type=MESH,
        )

    def own_copy(s, t):
        rows_at, cols_at = place(s, t)
        return pltpu.make_async_copy(
            total.at[s, :, cols_at], own_hbm.at[rows_at, cols_at],
            own_sem.at[lax.rem(s, share), t],
        )

    def score(shards, c):
        x = jnp.concatenate([gathered[s, c] for s in shards], axis=0)

        def one(t, carry):
            at = pl.ds(pl.multiple_of(t * TILE, TILE), TILE)
            y = mm_t(x, train[c, at, :])
            for j, s in enumerate(shards):
                total[s, :, at] += y[j * rows:(j + 1) * rows]

            @pl.when(c == CHUNKS - 1)
            def _():
                for s in shards:
                    @pl.when(s // share != layer)
                    def _():
                        sent[s, t] = total[s, :, at].astype(BF16)
                        ex_copy(s, t).start()

                    @pl.when(s // share == layer)
                    def _():
                        own_copy(s, t).start()

            return carry

        lax.fori_loop(0, seqs // TILE, one, 0)

    for copy in train_copies:
        copy.wait()

    if n_blk == 1:
        for c in range(CHUNKS):
            score([z], c)

    if n_blk > 1:
        @pl.when((z == 0) | (z == n_blk - 1))
        def _():
            near = 1 + (z // (n_blk - 1)) * (n_blk - 3)
            down_raw.wait_recv()
            turn(raw, near, lambda c: None)

            def close(c, carry):
                score([z, near], c)
                return carry

            lax.fori_loop(0, CHUNKS, close, 0)

    def step(i, carry):
        far = 1 + i // CHUNKS
        c = lax.rem(i, CHUNKS)
        above, below = z + far, z - far
        from_above = (above < n_blk) & (z + far > 1)
        from_below = (below >= 0) & (n_blk - 1 - z + far > 1)

        @pl.when(from_above)
        def _():
            down_copy(above, c).wait_recv()

            @pl.when(z > 0)
            def _():
                down_copy(above, c).start()

        @pl.when(from_below)
        def _():
            up_copy(below, c).wait_recv()

            @pl.when(z < n_blk - 1)
            def _():
                up_copy(below, c).start()

        if n_blk > 2:
            @pl.when((far == 1) & from_above & from_below)
            def _():
                score([z, above, below], c)

        @pl.when(from_above & (far > 1))
        def _():
            score([above], c)

        @pl.when(from_below & (far > 1))
        def _():
            score([below], c)

        return carry

    lax.fori_loop(0, (n_blk - 1) * CHUNKS, step, 0)

    for copy in pack_copies:
        copy.wait_send()

    @pl.when(z == 1)
    def _():
        down_raw.wait_send()

    @pl.when(z == n_blk - 2)
    def _():
        up_raw.wait_send()

    def drain(i, carry):
        s, c = i // CHUNKS, lax.rem(i, CHUNKS)

        @pl.when((s >= z) & (z > 0) & (s + z > 2))
        def _():
            down_copy(s, c).wait_send()

        @pl.when((s <= z) & (z < n_blk - 1) & (2 * (n_blk - 1) - s - z > 2))
        def _():
            up_copy(s, c).wait_send()

        return carry

    lax.fori_loop(0, n_blk * CHUNKS, drain, 0)

    def drain_ex(i, carry):
        s, t = i // tiles, lax.rem(i, tiles)

        @pl.when(s // share != layer)
        def _():
            ex_copy(s, t).wait_send()

        @pl.when(s // share == layer)
        def _():
            own_copy(s, t).wait()
            for slot in range(n_layer - 1):
                pltpu.make_async_remote_copy(
                    src_ref=sent.at[s, t], dst_ref=got_hbm.at[(slot, *place(s, t))],
                    send_sem=ex_send.at[s, t],
                    recv_sem=ex_recv.at[slot, lax.rem(s, share), t],
                    device_id={"layer": lax.rem(layer + 1, n_layer)}, device_id_type=MESH,
                ).wait_recv()

        return carry

    tiles = seqs // TILE
    lax.fori_loop(0, n_blk * tiles, drain_ex, 0)


def body(n_blk, n_rep, n_layer, train_grads, queries, bases, eigenvalues):
    seqs, flat = train_grads.shape[1:]
    rows = queries.shape[2]
    k = bases.shape[2] // 2
    n_peer = n_blk * n_rep
    packet_rows = -(-(bases.shape[1] + eigenvalues.shape[1] // LANES) // 8) * 8
    share = n_blk // n_layer
    cols = flat // CHUNKS
    tiles = seqs // TILE
    hbm = pl.BlockSpec(memory_space=pltpu.HBM)
    dma = pltpu.SemaphoreType.DMA
    own, got = pl.pallas_call(
        functools.partial(kernel, n_blk, n_rep, n_layer),
        out_shape=(
            jax.ShapeDtypeStruct((share * rows, seqs), F32),
            jax.ShapeDtypeStruct((max(n_layer - 1, 1), share * rows, seqs), BF16),
        ),
        in_specs=[hbm] * 4,
        out_specs=(hbm, hbm),
        scratch_shapes=[
            pltpu.VMEM(bases.shape[1:], BF16),
            pltpu.VMEM(eigenvalues.shape, F32),
            pltpu.VMEM((CHUNKS, seqs, cols), BF16),
            pltpu.VMEM((rows, flat), BF16),
            pltpu.VMEM((rows, flat), BF16),
            pltpu.VMEM((packet_rows, LANES), F32),
            pltpu.VMEM((n_peer, packet_rows, LANES), F32),
            pltpu.VMEM((k, 2 * k), F32),
            pltpu.VMEM((flat // LANES, LANES), F32),
            pltpu.VMEM((rows * flat // LANES, LANES), F32),
            pltpu.VMEM((n_blk, CHUNKS, rows, cols), BF16),
            pltpu.VMEM((n_blk, rows, seqs), F32),
            pltpu.VMEM((n_blk, tiles, rows, TILE), BF16),
            dma((CHUNKS,)),
            dma,
            dma,
            dma,
            dma((n_peer,)),
            dma((n_peer,)),
            dma((2,)),
            dma,
            dma((n_blk, CHUNKS)),
            dma((n_blk, CHUNKS)),
            dma((n_blk, CHUNKS)),
            dma((n_blk, CHUNKS)),
            dma((n_blk, tiles)),
            dma((n_layer, share, tiles)),
            dma((share, tiles)),
        ],
        compiler_params=pltpu.CompilerParams(
            collective_id=0, has_side_effects=True, vmem_limit_bytes=63 * 2**20
        ),
        name="influence",
    )(train_grads, queries, bases, eigenvalues)
    for slot in range(n_layer - 1):
        own = own + got[slot].astype(F32)
    return own[None]


def solution(mesh):
    sizes = mesh.shape
    return jax.shard_map(
        functools.partial(body, sizes["blk"], sizes["rep"], sizes["layer"]),
        mesh=mesh,
        in_specs=(
            P("layer", ("groups", "blk"), None),
            P("layer", "rep", ("groups", "blk"), None),
            P("layer", ("blk", "rep"), None),
            P("layer", ("blk", "rep")),
        ),
        out_specs=P("rep", "layer", ("groups", "blk")),
        check_vma=False,
    )
```

```python
import functools
import jax
import jax.numpy as jnp
from jax import lax
from jax.experimental import pallas as pl
from jax.experimental.pallas import tpu as pltpu
from jax.sharding import PartitionSpec as P

MESH = pl.DeviceIdType.MESH
F32 = jnp.float32
BF16 = jnp.bfloat16
LANES = 128
CHUNKS = 4
TILE = 256


def mm(a, b):
    return jnp.dot(a, b, preferred_element_type=F32)


def mm_t(a, b):
    return lax.dot_general(a, b, (((1,), (1,)), ((), ())), preferred_element_type=F32)


def one_hot(cond):
    return jnp.where(cond, 1.0, 0.0).astype(BF16)


def iota(shape, dim):
    return lax.broadcasted_iota(jnp.int32, shape, dim)


def kernel(
    n_blk, n_rep, n_layer,
    train_hbm, query_hbm, bases_hbm, eigen_hbm, out_hbm,
    bases_ref, eigen_ref, train, query, raw, packet, packets, basis, eigen, square, gathered,
    total, sent, got,
    train_sem, query_sem, bases_sem, eigen_sem, pack_send, pack_recv, raw_send, raw_recv,
    up_send, up_recv, down_send, down_recv, ex_send, ex_recv, out_sem,
):
    z = lax.axis_index("blk")
    rep = lax.axis_index("rep")
    layer = lax.axis_index("layer")
    n_peer = n_blk * n_rep
    me = z * n_rep + rep
    basis_rows = bases_ref.shape[0]
    eigen_rows = eigen_ref.shape[1] // LANES
    rows, flat = query.shape
    k = basis.shape[0]
    cols = flat // CHUNKS
    seqs = train.shape[1]
    share = n_blk // n_layer
    pairs = flat // LANES
    width = 2 * LANES

    bases_copy = pltpu.make_async_copy(bases_hbm.at[0], bases_ref, bases_sem)
    bases_copy.start()
    eigen_copy = pltpu.make_async_copy(eigen_hbm, eigen_ref, eigen_sem)
    eigen_copy.start()
    query_copy = pltpu.make_async_copy(query_hbm.at[0, 0], query, query_sem)
    query_copy.start()
    train_copies = [
        pltpu.make_async_copy(
            train_hbm.at[0, :, pl.ds(c * cols, cols)], train.at[c], train_sem.at[c]
        )
        for c in range(CHUNKS)
    ]

    barrier = pltpu.get_barrier_semaphore()
    peers = []
    for d in range(1, n_peer):
        peer = lax.rem(me + d, n_peer)
        peers.append({"blk": peer // n_rep, "rep": lax.rem(peer, n_rep)})
    for peer in peers:
        pl.semaphore_signal(barrier, inc=1, device_id=peer, device_id_type=MESH)
    for d in range(1, n_layer):
        pl.semaphore_signal(
            barrier, inc=1, device_id={"layer": lax.rem(layer + d, n_layer)}, device_id_type=MESH
        )

    packet[...] = jnp.zeros_like(packet)
    bases_copy.wait()
    eigen_copy.wait()
    packet[0:basis_rows, :] = bases_ref[...].astype(F32)
    for j in range(eigen_rows):
        packet[basis_rows + j:basis_rows + j + 1, :] = eigen_ref[:, j * LANES:(j + 1) * LANES]
    pl.semaphore_wait(barrier, n_peer - 1 + n_layer - 1)

    pack_copies = []
    for d in range(1, n_peer):
        copy = pltpu.make_async_remote_copy(
            src_ref=packet, dst_ref=packets.at[me],
            send_sem=pack_send.at[d], recv_sem=pack_recv.at[d],
            device_id=peers[d - 1], device_id_type=MESH,
        )
        copy.start()
        pack_copies.append(copy)
    packets[me] = packet[...]

    def raw_copy(side, to):
        return pltpu.make_async_remote_copy(
            src_ref=query_hbm.at[0, 0], dst_ref=raw,
            send_sem=raw_send.at[side], recv_sem=raw_recv,
            device_id={"blk": to}, device_id_type=MESH,
        )

    down_raw = raw_copy(0, lax.rem(z + n_blk - 1, n_blk))
    up_raw = raw_copy(1, lax.rem(z + 1, n_blk))

    @pl.when(z == 1)
    def _():
        down_raw.start()

    @pl.when(z == n_blk - 2)
    def _():
        up_raw.start()

    for copy in train_copies:
        copy.start()
    total[...] = jnp.zeros_like(total)

    wide_row, wide_col = iota((width, width), 0), iota((width, width), 1)
    row_k, col_k = iota((width, k), 0), iota((width, k), 1)
    pick_u = one_hot(col_k == 2 * (row_k & (pairs - 1)) + row_k // LANES)
    pick_v = one_hot(col_k == (row_k & (k - 1)))
    same_u = (wide_row & (LANES - 1)) // pairs == (wide_col & (LANES - 1)) // pairs
    same_v = wide_row // k == wide_col // k

    for copy in pack_copies:
        copy.wait_recv()
    for i in range(n_peer):
        basis[i * basis_rows:(i + 1) * basis_rows, :] = packets[i, 0:basis_rows, :]
        eigen[i * eigen_rows:(i + 1) * eigen_rows, :] = packets[
            i, basis_rows:basis_rows + eigen_rows, :
        ]

    u = basis[:, 0:k].astype(BF16)
    v = basis[:, k:2 * k].astype(BF16)

    def spread(pick, left, same):
        return jnp.where(same, mm_t(left, pick), 0.0).astype(BF16)

    u_turn = spread(pick_u, mm(pick_u, u).astype(BF16), same_u)
    u_back = spread(pick_u, mm_t(pick_u, u).astype(BF16), same_u)
    v_turn = spread(pick_v, mm(pick_v, v).astype(BF16), same_v)
    v_back = spread(pick_v, mm_t(pick_v, v).astype(BF16), same_v)

    eig = eigen[...]
    inverse = 1.0 / (eig + 0.1 * (jnp.sum(eig) / flat))
    group = LANES // pairs
    inverse_t = jnp.concatenate([inverse] * group, axis=0).T
    inverse_t = jnp.concatenate([inverse_t[0:k], inverse_t[k:2 * k]], axis=1)
    batch = 4
    inverse_t = jnp.concatenate([inverse_t] * batch, axis=0)

    def up_copy(s, c):
        return pltpu.make_async_remote_copy(
            src_ref=gathered.at[s, c], dst_ref=gathered.at[s, c],
            send_sem=up_send.at[s, c], recv_sem=up_recv.at[s, c],
            device_id={"blk": lax.rem(z + 1, n_blk)}, device_id_type=MESH,
        )

    def down_copy(s, c):
        return pltpu.make_async_remote_copy(
            src_ref=gathered.at[s, c], dst_ref=gathered.at[s, c],
            send_sem=down_send.at[s, c], recv_sem=down_recv.at[s, c],
            device_id={"blk": lax.rem(z + n_blk - 1, n_blk)}, device_id_type=MESH,
        )

    def turn(source, s, on_chunk):
        for c in range(flat // width):
            half = mm(source[:, c * width:(c + 1) * width], v_turn).astype(BF16).astype(F32)
            for j in range(2):
                square[pl.ds(2 * c + j, rows, stride=pairs), :] = half[:, j * LANES:(j + 1) * LANES]
        for b in range(rows // group // batch):
            stack = []
            for g in range(batch):
                at = (b * batch + g) * LANES
                t = square[at:at + LANES, :].T
                stack.append(jnp.concatenate([t[0:k], t[k:2 * k]], axis=1))
            a = jnp.concatenate(stack, axis=0).astype(BF16)
            scaled = (mm(a, u_turn) * inverse_t).astype(BF16)
            back = mm(scaled, u_back)
            for g in range(batch):
                at = (b * batch + g) * LANES
                part = back[g * k:(g + 1) * k]
                square[at:at + LANES, :] = jnp.concatenate(
                    [part[:, 0:LANES], part[:, LANES:width]], axis=0
                ).T
        per_chunk = cols // width
        for c in range(flat // width):
            x = jnp.concatenate(
                [square[pl.ds(2 * c + j, rows, stride=pairs), :] for j in range(2)], axis=1
            ).astype(BF16)
            at = (c % per_chunk) * width
            gathered[s, c // per_chunk, :, at:at + width] = mm(x, v_back).astype(BF16)
            if c % per_chunk == per_chunk - 1:
                on_chunk(c // per_chunk)

    def send_own(c):
        @pl.when(z > 1)
        def _():
            down_copy(z, c).start()

        @pl.when(z < n_blk - 2)
        def _():
            up_copy(z, c).start()

    query_copy.wait()
    turn(query, z, send_own)

    def ex_copy(s, t):
        return pltpu.make_async_remote_copy(
            src_ref=sent.at[s, t], dst_ref=got.at[layer, lax.rem(s, share), t],
            send_sem=ex_send.at[s, t], recv_sem=ex_recv.at[layer, lax.rem(s, share), t],
            device_id={"layer": s // share}, device_id_type=MESH,
        )

    def score(shards, c):
        x = jnp.concatenate([gathered[s, c] for s in shards], axis=0).T

        def one(t, carry):
            at = pl.ds(pl.multiple_of(t * TILE, TILE), TILE)
            y = mm(train[c, at, :], x).T
            for j, s in enumerate(shards):
                total[s, :, at] += y[j * rows:(j + 1) * rows]

            @pl.when(c == CHUNKS - 1)
            def _():
                for s in shards:
                    @pl.when(s // share != layer)
                    def _():
                        sent[s, t] = total[s, :, at].astype(BF16)
                        ex_copy(s, t).start()

            return carry

        lax.fori_loop(0, seqs // TILE, one, 0)

    for copy in train_copies:
        copy.wait()

    if n_blk == 1:
        for c in range(CHUNKS):
            score([z], c)

    if n_blk > 1:
        @pl.when((z == 0) | (z == n_blk - 1))
        def _():
            near = 1 + (z // (n_blk - 1)) * (n_blk - 3)
            down_raw.wait_recv()
            turn(raw, near, lambda c: None)

            def close(c, carry):
                score([z, near], c)
                return carry

            lax.fori_loop(0, CHUNKS, close, 0)

    def step(i, carry):
        far = 1 + i // CHUNKS
        c = lax.rem(i, CHUNKS)
        above, below = z + far, z - far
        from_above = (above < n_blk) & (z + far > 1)
        from_below = (below >= 0) & (n_blk - 1 - z + far > 1)

        @pl.when(from_above)
        def _():
            down_copy(above, c).wait_recv()

            @pl.when(z > 0)
            def _():
                down_copy(above, c).start()

        @pl.when(from_below)
        def _():
            up_copy(below, c).wait_recv()

            @pl.when(z < n_blk - 1)
            def _():
                up_copy(below, c).start()

        if n_blk > 2:
            @pl.when((far == 1) & from_above & from_below)
            def _():
                score([z, above, below], c)

        @pl.when(from_above & (far > 1))
        def _():
            score([above], c)

        @pl.when(from_below & (far > 1))
        def _():
            score([below], c)

        return carry

    lax.fori_loop(0, (n_blk - 1) * CHUNKS, step, 0)

    for copy in pack_copies:
        copy.wait_send()

    @pl.when(z == 1)
    def _():
        down_raw.wait_send()

    @pl.when(z == n_blk - 2)
    def _():
        up_raw.wait_send()

    def drain(i, carry):
        s, c = i // CHUNKS, lax.rem(i, CHUNKS)

        @pl.when((s >= z) & (z > 0) & (s + z > 2))
        def _():
            down_copy(s, c).wait_send()

        @pl.when((s <= z) & (z < n_blk - 1) & (2 * (n_blk - 1) - s - z > 2))
        def _():
            up_copy(s, c).wait_send()

        return carry

    lax.fori_loop(0, n_blk * CHUNKS, drain, 0)

    tiles = seqs // TILE
    high = (2 * z) // n_blk

    def out_copy(at, t):
        span = pl.ds(pl.multiple_of(t * TILE, TILE), TILE)
        return pltpu.make_async_copy(
            total.at[layer * share + at, :, span],
            out_hbm.at[pl.ds(pl.multiple_of(at * rows, rows), rows), span],
            out_sem.at[at, t],
        )

    def collect(i, carry):
        at, t = i // tiles, lax.rem(i, tiles)
        at = at + high * (share - 1 - 2 * at)
        span = pl.ds(pl.multiple_of(t * TILE, TILE), TILE)
        mine = layer * share + at
        for other in range(n_layer):
            @pl.when(layer != other)
            def _():
                pltpu.make_async_remote_copy(
                    src_ref=sent.at[0, 0], dst_ref=got.at[other, at, t],
                    send_sem=ex_send.at[0, 0], recv_sem=ex_recv.at[other, at, t],
                    device_id={"layer": other}, device_id_type=MESH,
                ).wait_recv()
                total[mine, :, span] += got[other, at, t].astype(F32)
        out_copy(at, t).start()
        return carry

    lax.fori_loop(0, share * tiles, collect, 0)

    def drain_out(i, carry):
        out_copy(i // tiles, lax.rem(i, tiles)).wait()
        return carry

    lax.fori_loop(0, share * tiles, drain_out, 0)
    def drain_ex(i, carry):
        s, t = i // tiles, lax.rem(i, tiles)

        @pl.when(s // share != layer)
        def _():
            ex_copy(s, t).wait_send()

        return carry

    lax.fori_loop(0, n_blk * tiles, drain_ex, 0)


def body(n_blk, n_rep, n_layer, train_grads, queries, bases, eigenvalues):
    seqs, flat = train_grads.shape[1:]
    rows = queries.shape[2]
    k = bases.shape[2] // 2
    n_peer = n_blk * n_rep
    packet_rows = -(-(bases.shape[1] + eigenvalues.shape[1] // LANES) // 8) * 8
    share = n_blk // n_layer
    cols = flat // CHUNKS
    tiles = seqs // TILE
    hbm = pl.BlockSpec(memory_space=pltpu.HBM)
    dma = pltpu.SemaphoreType.DMA
    out = pl.pallas_call(
        functools.partial(kernel, n_blk, n_rep, n_layer),
        out_shape=jax.ShapeDtypeStruct((share * rows, seqs), F32),
        in_specs=[hbm] * 4,
        out_specs=hbm,
        scratch_shapes=[
            pltpu.VMEM(bases.shape[1:], BF16),
            pltpu.VMEM(eigenvalues.shape, F32),
            pltpu.VMEM((CHUNKS, seqs, cols), BF16),
            pltpu.VMEM((rows, flat), BF16),
            pltpu.VMEM((rows, flat), BF16),
            pltpu.VMEM((packet_rows, LANES), F32),
            pltpu.VMEM((n_peer, packet_rows, LANES), F32),
            pltpu.VMEM((k, 2 * k), F32),
            pltpu.VMEM((flat // LANES, LANES), F32),
            pltpu.VMEM((rows * flat // LANES, LANES), F32),
            pltpu.VMEM((n_blk, CHUNKS, rows, cols), BF16),
            pltpu.VMEM((n_blk, rows, seqs), F32),
            pltpu.VMEM((n_blk, tiles, rows, TILE), BF16),
            pltpu.VMEM((n_layer, share, tiles, rows, TILE), BF16),
            dma((CHUNKS,)),
            dma,
            dma,
            dma,
            dma((n_peer,)),
            dma((n_peer,)),
            dma((2,)),
            dma,
            dma((n_blk, CHUNKS)),
            dma((n_blk, CHUNKS)),
            dma((n_blk, CHUNKS)),
            dma((n_blk, CHUNKS)),
            dma((n_blk, tiles)),
            dma((n_layer, share, tiles)),
            dma((share, tiles)),
        ],
        compiler_params=pltpu.CompilerParams(
            collective_id=0, has_side_effects=True, vmem_limit_bytes=63 * 2**20
        ),
        name="influence",
    )(train_grads, queries, bases, eigenvalues)
    return out[None]


def solution(mesh):
    sizes = mesh.shape
    return jax.shard_map(
        functools.partial(body, sizes["blk"], sizes["rep"], sizes["layer"]),
        mesh=mesh,
        in_specs=(
            P("layer", ("groups", "blk"), None),
            P("layer", "rep", ("groups", "blk"), None),
            P("layer", ("blk", "rep"), None),
            P("layer", ("blk", "rep")),
        ),
        out_specs=P("rep", "layer", ("groups", "blk")),
        check_vma=False,
    )
```
